256 devices in a mesh: space: 8 (over y, core), tm: 32 (over x, z).
Axes of the slice: x: 4, y: 4, z: 8, core: 2. Of those that a mesh axis runs over, the one named last changes fastest.
Arguments:
- factors: float32 [2048, 131072], P('tm', 'space'), as said below
Outputs:
- merged: float32 [64, 131072], P(None, ('space', 'tm'))
Inputs may be any that keep to these rules, and one draw needn't show every extreme that they name: `factors`: each block of 64 rows is a scaled left factor of one block of snapshots.
All inputs are finite; a program needn't handle non-finite values.
Results may differ from the reference program's by a relative error of at most 0.0003.
Values sent between devices are 32-bit elements; how exact they have to be, the bound alone decides.
No kernel may reach another device: no remote copies, remote signals or barrier semaphores. Data moves between devices by JAX's collectives and lax.ppermute only.
A program may use at most 64 MiB of HBM per device.

```python
import jax
import jax.numpy as jnp
from jax import lax

K = 64
ITERS = 3
GRID = 131072
BLOCKS = 32
LEVELS = 5


def draw_factors(key, part):
    key = jax.random.fold_in(key, 11)
    key_scale, key_modes, key_mix, key_noise = jax.random.split(key, 4)
    scales = jnp.exp(jax.random.uniform(key_scale, (K,), jnp.float32, jnp.log(0.3), jnp.log(3.0)))
    modes = jax.random.normal(key_modes, (K, GRID), jnp.float32) * scales[:, None]
    noise = jax.random.normal(key_noise, (BLOCKS, K, GRID), jnp.float32) * 0.03
    mixing = jax.random.normal(key_mix, (BLOCKS, K, K), jnp.float32) * (K * BLOCKS) ** (-0.5)
    mixed = jnp.einsum('jab,bm->jam', mixing, modes)
    return (mixed + noise).reshape(BLOCKS * K, GRID).astype(jnp.float32)


def setup_inputs(seed: int = 0) -> dict:
    splits = jax.random.split(jax.random.key(seed), 2)
    return {
        "factors": draw_factors(jax.random.fold_in(splits[1], 71), 0),
    }


def subspace(gram):
    size = gram.shape[0]
    basis = jnp.eye(size, size // 2, dtype=jnp.float32)
    for step in range(ITERS):
        image = jnp.dot(gram, basis, precision=lax.Precision.HIGHEST)
        inner = jnp.dot(image.T, image, precision=lax.Precision.HIGHEST)
        lower_factor = jnp.linalg.cholesky(inner)
        basis = lax.linalg.triangular_solve(lower_factor, image, left_side=False, lower=True, transpose_a=True)
    return basis

def merge_pair(stacked):
    gram = jnp.dot(stacked, stacked.T, precision=lax.Precision.HIGHEST)
    basis = subspace(gram)
    return jnp.dot(basis.T, stacked, precision=lax.Precision.HIGHEST)

def reference(factors):
    level_set = factors.reshape(BLOCKS, K, GRID)
    for level in range(LEVELS):
        count = level_set.shape[0] // 2
        paired = level_set.reshape(count, 2 * K, GRID)
        level_set = lax.map(merge_pair, paired)
    return level_set[0]
```

```python
import jax
import jax.numpy as jnp
from jax import lax
from jax.experimental import pallas as pl
from jax.experimental.pallas import tpu as pltpu
from jax.sharding import Mesh
from jax.sharding import PartitionSpec as P

ITERS = 3
RANK = 64
REACH = 4
ROWS_CONTRACT = (((1,), (1,)), ((), ()))
HIGHEST = lax.Precision.HIGHEST
F32 = jnp.float32
BF16 = jnp.bfloat16


def call(kernel, name, shapes, *operands, scratch=(), anywhere=False):
    space = pl.ANY if anywhere else pltpu.VMEM
    spec = pl.BlockSpec(memory_space=space)
    return pl.pallas_call(
        kernel,
        out_shape=[jax.ShapeDtypeStruct(shape, F32) for shape in shapes],
        in_specs=[spec] * len(operands),
        out_specs=[spec] * len(shapes),
        scratch_shapes=list(scratch),
        compiler_params=pltpu.CompilerParams(vmem_limit_bytes=40 * 1024 * 1024),
        name=name,
    )(*operands)


def exact(left, right):
    return jnp.dot(left, right, precision=HIGHEST, preferred_element_type=F32)


def exact_rows(left, right):
    return lax.dot_general(
        left, right, ROWS_CONTRACT, precision=HIGHEST, preferred_element_type=F32
    )


def part(value):
    high = value.astype(BF16)
    return high, value - high.astype(F32)


def product(left, right):
    left_high, left_rest = part(left)
    right_high, right_rest = part(right)

    def dot(a, b):
        return jnp.dot(a, b, preferred_element_type=F32)

    return dot(left_high, right_high) + (
        dot(left_high, right_rest.astype(BF16)) + dot(left_rest.astype(BF16), right_high)
    )


def gram_terms(rows):
    high, rest = part(rows)
    middle, rest = part(rest)
    low = rest.astype(BF16)

    def dot(a, b):
        return lax.dot_general(a, b, ROWS_CONTRACT, preferred_element_type=F32)

    return dot(high, high) + dot(middle, middle), dot(high, middle) + dot(high, low)


def splat_lane(block, lane):
    return jnp.broadcast_to(block[:, lane : lane + 1], (8, 128))


def splat_row(block, row):
    return jnp.broadcast_to(block[row : row + 1, :], (8, 128))


def orthonormal(images):
    rank = images[0].shape[0]
    blocks = rank // 8
    row = lax.broadcasted_iota(jnp.int32, (8, 128), 0)
    pad = jnp.zeros((128 - rank, 128), F32)
    inner = [exact_rows(image, jnp.concatenate([image, pad], 0)) for image in images]
    inners = [[s[8 * i : 8 * i + 8] for i in range(blocks)] for s in inner]
    targets = [[z[8 * i : 8 * i + 8] for i in range(blocks)] for z in images]
    results = [[None] * blocks for _ in images]
    for k in range(blocks):
        columns = [
            [
                [splat_lane(s[i], 8 * k + j) for j in range(8)] if i >= k else None
                for i in range(blocks)
            ]
            for s in inners
        ]
        pivots = [jnp.ones((8, 128), F32) for _ in images]
        last = k == blocks - 1
        for j in range(8):
            for n in range(len(images)):
                s, z, c = inners[n], targets[n], columns[n]
                pivot = splat_row(c[k][j], j)
                inverse = 1.0 / pivot
                pivots[n] = jnp.where(row == j, pivot, pivots[n])
                row_s = None if last else splat_row(s[k], j) * inverse
                row_z = splat_row(z[k], j) * inverse
                row_c = [splat_row(c[k][m], j) * inverse if m > j else None for m in range(8)]
                for i in range(k, blocks):
                    if i == k and j == 7:
                        continue
                    weight = jnp.where(row > j, c[i][j], 0.0) if i == k else c[i][j]
                    if not last:
                        s[i] = s[i] - weight * row_s
                    z[i] = z[i] - weight * row_z
                    for m in range(j + 1, 8):
                        c[i][m] = c[i][m] - weight * row_c[m]
        for n in range(len(images)):
            results[n][k] = targets[n][k] * lax.rsqrt(pivots[n])
    return [jnp.concatenate(result, 0) for result in results]


def bases(grams):
    first = tuple(orthonormal([gram[:RANK] for gram in grams]))

    def step(_, found):
        return tuple(orthonormal([exact(x, gram) for x, gram in zip(found, grams)]))

    return lax.fori_loop(0, ITERS - 1, step, first)


def two_levels(gram):
    pair = 2 * RANK
    left, right = bases([gram[:pair, :pair], gram[pair:, pair:]])
    cross = exact_rows(exact(left, gram[:pair, pair:]), right)
    upper = exact_rows(exact(left, gram[:pair, :pair]), left)
    lower = exact_rows(exact(right, gram[pair:, pair:]), right)
    (top,) = bases(
        [
            jnp.concatenate(
                [
                    jnp.concatenate([upper, cross], 1),
                    jnp.concatenate([cross.T, lower], 1),
                ],
                0,
            )
        ]
    )
    return jnp.concatenate([exact(top[:, :RANK], left), exact(top[:, RANK:], right)], 1)


def signs():
    where = lax.axis_index("z")
    odd = lax.rem(where, 2)
    return where, odd, 2 * odd - 1


def pack(factor, mine, width):
    def kernel(source, target, sems):
        where, odd, sign = signs()
        first = where if mine else where + 1 - 2 * odd
        step = sign if mine else -sign
        copies = []
        for d in range(REACH):
            chunk = lax.rem(first + step * d + 8, 8)
            for x in range(4):
                start = pl.multiple_of((x * 8 + chunk) * width, width)
                copies.append(
                    pltpu.make_async_copy(
                        source.at[:, pl.ds(start, width)],
                        target.at[d, :, pl.ds(x * width, width)],
                        sems.at[d * 4 + x],
                    )
                )
        for copy in copies:
            copy.start()
        for copy in copies:
            copy.wait()

    (packed,) = call(
        kernel,
        "pack",
        [(REACH, RANK, 4 * width)],
        factor,
        scratch=[pltpu.SemaphoreType.DMA((REACH * 4,))],
        anywhere=True,
    )
    return packed


def pair_gram(own, other):
    def kernel(own_ref, other_ref, out_ref):
        symmetric = half = None
        for d in range(REACH):
            rows = jnp.concatenate([own_ref[d], other_ref[d]], 0)
            a, b = gram_terms(rows)
            symmetric = a if symmetric is None else symmetric + a
            half = b if half is None else half + b
        gram = symmetric + (half + half.T)
        out_ref[:, : 2 * RANK] = gram[:RANK]
        out_ref[:, 2 * RANK :] = gram[RANK:, RANK:]

    (gram,) = call(kernel, "pair_gram", [(RANK, 3 * RANK)], own, other)
    return gram


def pair_merge(here, there, own, other):
    width = own.shape[2]

    def kernel(here_ref, there_ref, own_ref, other_ref, *outs):
        where, odd, sign = signs()
        upper = odd == 1
        here = here_ref[...]
        there = there_ref[...]
        own_own = here[:, :RANK] + there[:, 2 * RANK :]
        cross = here[:, RANK : 2 * RANK] + there[:, RANK : 2 * RANK].T
        other_other = here[:, 2 * RANK :] + there[:, :RANK]
        top = jnp.where(upper, other_other, own_own)
        bottom = jnp.where(upper, own_own, other_other)
        cross = jnp.where(upper, cross.T, cross)
        gram = jnp.concatenate(
            [jnp.concatenate([top, cross], 1), jnp.concatenate([cross.T, bottom], 1)], 0
        )
        (basis,) = bases([gram])
        swapped = jnp.concatenate([basis[:, RANK:], basis[:, :RANK]], 1)
        weights = jnp.where(upper, swapped, basis)
        for d in range(REACH):
            outs[d][...] = product(weights, jnp.concatenate([own_ref[d], other_ref[d]], 0))

    return call(kernel, "pair_merge", [(RANK, width)] * REACH, here, there, own, other)


def quad_gram(pieces, place):
    rank, width = pieces[0].shape
    half = rank // 2

    def kernel(*refs):
        ins, (stack, keep, send, packed) = refs[:4], refs[4:]
        for n in range(4):
            start = pl.multiple_of(place(n) * rank, rank)
            stack[pl.ds(start, rank), :] = ins[n][...]
        symmetric, terms = gram_terms(stack[...])
        gram = symmetric + (terms + terms.T)
        at = 0
        for i in range(4):
            columns = (4 - i) * rank
            packed[:, at : at + columns] = gram[i * rank : (i + 1) * rank, i * rank :]
            at += columns
        core = lax.axis_index("c")
        keep[...] = packed[pl.ds(pl.multiple_of(core * half, half), half), :]
        send[...] = packed[pl.ds(pl.multiple_of((1 - core) * half, half), half), :]

    return call(
        kernel,
        "quad_gram",
        [(4 * rank, width), (half, 10 * rank), (half, 10 * rank)],
        *pieces,
        scratch=[pltpu.VMEM((rank, 10 * rank), F32)],
    )


def quad_merge(own_half, other_half, stack, split):
    rows, width = stack.shape
    share = width // 4 if split else width

    def kernel(own_ref, other_ref, stack_ref, *outs):
        core = lax.axis_index("c")
        first = core == 0
        own_half = own_ref[...]
        other_half = other_ref[...]
        packed = jnp.concatenate(
            [
                jnp.where(first, own_half, other_half),
                jnp.where(first, other_half, own_half),
            ],
            0,
        )
        at = 0
        found = {}
        for i in range(4):
            for j in range(i, 4):
                found[i, j] = packed[:, at : at + RANK]
                at += RANK
        for i in range(4):
            for j in range(i):
                found[i, j] = found[j, i].T
        gram = jnp.concatenate(
            [jnp.concatenate([found[i, j] for j in range(4)], 1) for i in range(4)], 0
        )
        weights = two_levels(gram)
        if not split:
            outs[0][...] = product(weights, stack_ref[...])
            return
        x = lax.axis_index("x")
        for s in range(4):
            start = pl.multiple_of((x ^ s) * share, share)
            outs[s][...] = product(weights, stack_ref[:, pl.ds(start, share)])

    return call(
        kernel,
        "quad_merge",
        [(RANK, share)] * (4 if split else 1),
        own_half,
        other_half,
        stack,
    )


def swap(block, axis, bits):
    count = lax.axis_size(axis)
    return lax.ppermute(block, axis, [(i, i ^ bits) for i in range(count)])


def outward(block, distance):
    route = [(i, (i + (distance if i % 2 else -distance)) % 8) for i in range(8)]
    return lax.ppermute(block, "z", route)


def sum_four(block, axis, unit):
    one, two, three = (swap(block, axis, unit * s) for s in (1, 2, 3))
    return (block + one) + (two + three)


def sum_core_halves(keep, send):
    return keep + swap(send, "c", 1)


def body(factor):
    width = factor.shape[1] // 32
    theirs = pack(factor, False, width)
    other = swap(theirs, "z", 1)
    own = pack(factor, True, width)

    gram = pair_gram(own, other)
    gram = gram + swap(gram, "c", 1)
    gram = sum_four(gram, "y", 1)
    merged = pair_merge(gram, swap(gram, "z", 1), own, other)

    pieces = [merged[0]] + [outward(merged[d], d) for d in range(1, REACH)]

    def place_z(n):
        where, odd, sign = signs()
        offset = (0, 1, -1, 2)[n]
        return lax.rem(lax.div(where, 2) + sign * offset + 8, 4)

    stack, keep, send = quad_gram(pieces, place_z)
    half = sum_core_halves(keep, send)
    half = sum_four(half, "y", 1)
    half = half + swap(half, "z", 1)
    half = sum_four(half, "z", 2)
    parts = quad_merge(half, swap(half, "c", 1), stack, True)

    pieces = [parts[0]] + [swap(parts[s], "x", s) for s in range(1, 4)]

    def place_x(n):
        return lax.axis_index("x") ^ n

    stack, keep, send = quad_gram(pieces, place_x)
    half = sum_core_halves(keep, send)
    half = sum_four(half, "y", 1)
    half = half + swap(half, "z", 1)
    half = sum_four(half, "z", 2)
    half = sum_four(half, "x", 1)
    (merged,) = quad_merge(half, swap(half, "c", 1), stack, False)
    return merged


def solution(mesh):
    split = Mesh(mesh.devices.reshape(4, 2, 4, 8), ("y", "c", "x", "z"))
    return jax.shard_map(
        body,
        mesh=split,
        in_specs=(P(("x", "z"), ("y", "c")),),
        out_specs=P(None, ("y", "c", "x", "z")),
        check_vma=False,
    )
```

```python
import jax
import jax.numpy as jnp
from jax import lax
from jax.experimental import pallas as pl
from jax.experimental.pallas import tpu as pltpu
from jax.sharding import Mesh
from jax.sharding import PartitionSpec as P

ITERS = 3
RANK = 64
ROWS_CONTRACT = (((1,), (1,)), ((), ()))
HIGHEST = lax.Precision.HIGHEST
F32 = jnp.float32
BF16 = jnp.bfloat16


def call(kernel, name, shapes, *operands, scratch=(), anywhere=False, waits=()):
    spec = pl.BlockSpec(memory_space=pl.ANY if anywhere else pltpu.VMEM)
    source = pl.BlockSpec(memory_space=pltpu.HBM) if anywhere else spec
    passing = [pl.BlockSpec(memory_space=pl.ANY)] * len(waits)
    ins, outs, passed = len(operands), len(shapes), len(waits)

    def run(*refs):
        kernel(*refs[:ins], *refs[ins + passed : ins + passed + outs], *refs[ins + 2 * passed + outs :])

    return pl.pallas_call(
        run,
        out_shape=[jax.ShapeDtypeStruct(shape, F32) for shape in shapes]
        + [jax.ShapeDtypeStruct(wait.shape, F32) for wait in waits],
        in_specs=[source] * ins + passing,
        out_specs=[spec] * outs + passing,
        input_output_aliases={ins + n: outs + n for n in range(passed)},
        scratch_shapes=list(scratch),
        compiler_params=pltpu.CompilerParams(vmem_limit_bytes=40 * 1024 * 1024),
        name=name,
    )(*operands, *waits)


def exact(left, right):
    return jnp.dot(left, right, precision=HIGHEST, preferred_element_type=F32)


def exact_rows(left, right):
    return lax.dot_general(
        left, right, ROWS_CONTRACT, precision=HIGHEST, preferred_element_type=F32
    )


def part(value):
    high = value.astype(BF16)
    return high, value - high.astype(F32)


def product(left, right):
    left_high, left_rest = part(left)
    right_high, right_rest = part(right)

    def dot(a, b):
        return jnp.dot(a, b, preferred_element_type=F32)

    return dot(left_high, right_high) + (
        dot(left_high, right_rest.astype(BF16)) + dot(left_rest.astype(BF16), right_high)
    )


def gram_terms(rows):
    high, rest = part(rows)
    middle, rest = part(rest)
    low = rest.astype(BF16)

    def dot(a, b):
        return lax.dot_general(a, b, ROWS_CONTRACT, preferred_element_type=F32)

    return dot(high, high) + dot(middle, middle), dot(high, middle) + dot(high, low)


def splat_lane(block, lane):
    return jnp.broadcast_to(block[:, lane : lane + 1], (8, 128))


def splat_row(block, row):
    return jnp.broadcast_to(block[row : row + 1, :], (8, 128))


def orthonormal(images):
    rank = images[0].shape[0]
    blocks = rank // 8
    row = lax.broadcasted_iota(jnp.int32, (8, 128), 0)
    pad = jnp.zeros((128 - rank, 128), F32)
    inner = [exact_rows(image, jnp.concatenate([image, pad], 0)) for image in images]
    inners = [[s[8 * i : 8 * i + 8] for i in range(blocks)] for s in inner]
    targets = [[z[8 * i : 8 * i + 8] for i in range(blocks)] for z in images]
    results = [[None] * blocks for _ in images]
    ahead = [None] * len(images)
    for k in range(blocks):
        last = k == blocks - 1
        columns = []
        for n, s in enumerate(inners):
            found = {i: [splat_lane(s[i], 8 * k + j) for j in range(8)] for i in range(k + 1, blocks)}
            if ahead[n] is None:
                ahead[n] = [splat_lane(s[k], 8 * k + j) for j in range(8)]
            found[k] = ahead[n]
            columns.append(found)
        if not last:
            ahead = [[splat_lane(s[k + 1], 8 * k + 8 + j) for j in range(8)] for s in inners]
        pivots = [jnp.ones((8, 128), F32) for _ in images]
        for j in range(8):
            for n in range(len(images)):
                s, z, c = inners[n], targets[n], columns[n]
                pivot = splat_row(c[k][j], j)
                inverse = 1.0 / pivot
                pivots[n] = jnp.where(row == j, pivot, pivots[n])
                row_s = None if last else splat_row(s[k], j) * inverse
                row_z = splat_row(z[k], j) * inverse
                row_c = [splat_row(c[k][m], j) * inverse if m > j else None for m in range(8)]
                for i in range(k, blocks):
                    if i == k and j == 7:
                        continue
                    weight = jnp.where(row > j, c[i][j], 0.0) if i == k else c[i][j]
                    if not last:
                        s[i] = s[i] - weight * row_s
                    z[i] = z[i] - weight * row_z
                    for m in range(j + 1, 8):
                        c[i][m] = c[i][m] - weight * row_c[m]
                if not last:
                    weight = c[k + 1][j] * inverse
                    for m in range(8):
                        ahead[n][m] = ahead[n][m] - weight * splat_row(c[k + 1][j], m)
        for n in range(len(images)):
            results[n][k] = targets[n][k] * lax.rsqrt(pivots[n])
    return [jnp.concatenate(result, 0) for result in results]


def bases(grams):
    first = tuple(orthonormal([gram[:RANK] for gram in grams]))

    def step(_, found):
        return tuple(orthonormal([exact(x, gram) for x, gram in zip(found, grams)]))

    return lax.fori_loop(0, ITERS - 1, step, first)


def two_levels(gram):
    pair = 2 * RANK
    left, right = bases([gram[:pair, :pair], gram[pair:, pair:]])
    cross = exact_rows(exact(left, gram[:pair, pair:]), right)
    upper = exact_rows(exact(left, gram[:pair, :pair]), left)
    lower = exact_rows(exact(right, gram[pair:, pair:]), right)
    both = jnp.concatenate(
        [jnp.concatenate([upper, cross], 1), jnp.concatenate([cross.T, lower], 1)], 0
    )
    (top,) = bases([both])
    weights = jnp.concatenate([exact(top[:, :RANK], left), exact(top[:, RANK:], right)], 1)
    return weights, exact_rows(exact(top, both), top)


def signs():
    where = lax.axis_index("z")
    odd = lax.rem(where, 2)
    return where, odd, 2 * odd - 1


def pack(factor, mine, width, groups):
    count = sum(len(group) for group in groups)

    def kernel(source, *refs):
        targets, sems = refs[:-1], refs[-1]
        where, odd, sign = signs()
        first = where if mine else where + 1 - 2 * odd
        step = sign if mine else -sign
        copies = []
        for target, group in zip(targets, groups):
            for at, d in enumerate(group):
                chunk = lax.rem(first + step * d + 8, 8)
                for x in range(4):
                    start = pl.multiple_of((x * 8 + chunk) * width, width)
                    copies.append(
                        pltpu.make_async_copy(
                            source.at[:, pl.ds(start, width)],
                            target.at[at, :, pl.ds(x * width, width)],
                            sems.at[len(copies)],
                        )
                    )
        for copy in copies:
            copy.start()
        for copy in copies:
            copy.wait()

    return call(
        kernel,
        "pack",
        [(len(group), RANK, 4 * width) for group in groups],
        factor,
        scratch=[pltpu.SemaphoreType.DMA((4 * count,))],
        anywhere=True,
    )


def after(block, arrival):
    def kernel():
        pass

    return call(kernel, "after", [], waits=(block, arrival))


def pair_gram(own, other, waits):
    count = len(own) + len(other)

    def kernel(*refs):
        out_ref = refs[-1]
        near, none, far = refs[len(own) : count]
        others = [near[0], near[1], none[0], far[0]]
        symmetric = half = None
        for a, b in zip(refs[: len(own)], others):
            terms = gram_terms(jnp.concatenate([a[0], b], 0))
            symmetric = terms[0] if symmetric is None else symmetric + terms[0]
            half = terms[1] if half is None else half + terms[1]
        gram = symmetric + (half + half.T)
        out_ref[:, : 2 * RANK] = gram[:RANK]
        out_ref[:, 2 * RANK :] = gram[RANK:, RANK:]

    return call(kernel, "pair_gram", [(RANK, 3 * RANK)], *own, *other, waits=waits)


def pair_solve(here, there, own, other, waits):
    width = own.shape[2]

    def kernel(here_ref, there_ref, own_ref, other_ref, basis_ref, merged_ref):
        where, odd, sign = signs()
        upper = odd == 1
        here = here_ref[...]
        there = there_ref[...]
        own_own = here[:, :RANK] + there[:, 2 * RANK :]
        cross = here[:, RANK : 2 * RANK] + there[:, RANK : 2 * RANK].T
        other_other = here[:, 2 * RANK :] + there[:, :RANK]
        top = jnp.where(upper, other_other, own_own)
        bottom = jnp.where(upper, own_own, other_other)
        cross = jnp.where(upper, cross.T, cross)
        gram = jnp.concatenate(
            [jnp.concatenate([top, cross], 1), jnp.concatenate([cross.T, bottom], 1)], 0
        )
        (basis,) = bases([gram])
        merged_gram = exact_rows(exact(basis, gram), basis)
        swapped = jnp.concatenate([basis[:, RANK:], basis[:, :RANK]], 1)
        weights = jnp.where(upper, swapped, basis)
        basis_ref[:, : 2 * RANK] = weights
        basis_ref[:, 2 * RANK :] = merged_gram
        rows = jnp.concatenate([own_ref[0], other_ref[0]], 0)
        merged_ref[:, :width] = product(weights, rows)
        merged_ref[:, width : width + RANK] = merged_gram
        merged_ref[:, width + RANK :] = jnp.zeros((RANK, RANK), F32)

    shapes = [(RANK, 3 * RANK), (RANK, width + 2 * RANK)]
    return call(kernel, "pair_solve", shapes, here, there, own, other, waits=waits)


def near_merge(weights, own, other):
    width = own[0].shape[2]

    def kernel(*refs):
        for n in range(3):
            rows = jnp.concatenate([refs[3 + n][0], refs[6 + n][0]], 0)
            refs[9 + n][...] = product(refs[n][:, : 2 * RANK], rows)

    return call(kernel, "near_merge", [(RANK, width)] * 3, *weights, *own, *other)


def quad_gram(pieces, grams, width, place):
    half = RANK // 2

    def kernel(*refs):
        ins, diagonals, (stack, diagonal, keep, send, packed) = refs[:4], refs[4:8], refs[8:]
        for n in range(4):
            start = pl.multiple_of(place(n) * RANK, RANK)
            stack[pl.ds(start, RANK), :] = ins[n][:, :width]
            lane = grams[n][1]
            diagonal[pl.ds(start, RANK), :] = diagonals[n][:, lane : lane + RANK]
        symmetric, terms = gram_terms(stack[...])
        gram = symmetric + (terms + terms.T)
        at = 0
        for i in range(3):
            columns = (3 - i) * RANK
            packed[:, at : at + columns] = gram[i * RANK : (i + 1) * RANK, (i + 1) * RANK :]
            at += columns
        core = lax.axis_index("c")
        keep[...] = packed[pl.ds(pl.multiple_of(core * half, half), half), :]
        send[...] = packed[pl.ds(pl.multiple_of((1 - core) * half, half), half), :]

    return call(
        kernel,
        "quad_gram",
        [(4 * RANK, width), (4 * RANK, RANK), (half, 6 * RANK), (half, 6 * RANK)],
        *pieces,
        *(gram for gram, _ in grams),
        scratch=[pltpu.VMEM((RANK, 6 * RANK), F32)],
    )


def quad_merge(own_half, other_half, diagonal, stack, split):
    rows, width = stack.shape
    share = width // 4 if split else width

    def kernel(own_ref, other_ref, diagonal_ref, stack_ref, *outs):
        core = lax.axis_index("c")
        first = core == 0
        own_half = own_ref[...]
        other_half = other_ref[...]
        packed = jnp.concatenate(
            [
                jnp.where(first, own_half, other_half),
                jnp.where(first, other_half, own_half),
            ],
            0,
        )
        at = 0
        found = {}
        for i in range(4):
            found[i, i] = diagonal_ref[i * RANK : (i + 1) * RANK, :]
            for j in range(i + 1, 4):
                found[i, j] = packed[:, at : at + RANK]
                found[j, i] = found[i, j].T
                at += RANK
        gram = jnp.concatenate(
            [jnp.concatenate([found[i, j] for j in range(4)], 1) for i in range(4)], 0
        )
        weights, merged_gram = two_levels(gram)
        if not split:
            outs[0][...] = product(weights, stack_ref[...])
            return
        x = lax.axis_index("x")
        for s in range(4):
            start = pl.multiple_of((x ^ s) * share, share)
            outs[s][:, :share] = product(weights, stack_ref[:, pl.ds(start, share)])
            outs[s][:, share : share + RANK] = merged_gram
            outs[s][:, share + RANK :] = jnp.zeros((RANK, RANK), F32)

    shapes = [(RANK, share + 2 * RANK)] * 4 if split else [(RANK, share)]
    return call(kernel, "quad_merge", shapes, own_half, other_half, diagonal, stack)


def swap(block, axis, bits):
    count = lax.axis_size(axis)
    return lax.ppermute(block, axis, [(i, i ^ bits) for i in range(count)])


def outward(block, distance):
    route = [(i, (i + (distance if i % 2 else -distance)) % 8) for i in range(8)]
    return lax.ppermute(block, "z", route)


def sum_four(block, axis, unit):
    one, two, three = (swap(block, axis, unit * s) for s in (1, 2, 3))
    return (block + one) + (two + three)


def body(factor):
    width = factor.shape[1] // 32
    near, far, none = pack(factor, False, width, [(1, 2), (3,), (0,)])
    other_near = swap(near, "z", 1)
    other_far = swap(far, "z", 1)
    none, other_far = after(none, other_far)
    other_none = swap(none, "z", 1)
    own_one, own_two, own_none, own_far = pack(factor, True, width, [(1,), (2,), (0,), (3,)])
    first_own = outward(own_one, 1)
    relay_own = outward(own_two, 1)
    from_near = outward(other_near, 1)

    gram, first_own, relay_own = pair_gram(
        [own_one, own_two, own_none, own_far],
        [other_near, other_none, other_far],
        [first_own, relay_own],
    )
    second_own = swap(relay_own, "z", 1)
    gram = gram + swap(gram, "c", 1)
    gram = sum_four(gram, "y", 1)
    basis, far, from_near, second_own = pair_solve(
        gram, swap(gram, "z", 1), own_far, other_far, [from_near, second_own]
    )
    second_other = swap(from_near[1:], "z", 1)
    basis_one = outward(basis, 1)
    basis_two = outward(basis, 2)
    far = outward(far, 3)
    pieces = near_merge(
        [basis, basis_one, basis_two],
        [own_none, first_own, second_own],
        [other_none, from_near, second_other],
    )

    def place_z(n):
        where, odd, sign = signs()
        offset = (0, 1, -1, 2)[n]
        return lax.rem(lax.div(where, 2) + sign * offset + 8, 4)

    reach = 4 * width
    lane = 2 * RANK
    stack, diagonal, keep, send = quad_gram(
        [*pieces, far],
        [(basis, lane), (basis_one, lane), (basis_two, lane), (far, reach)],
        reach,
        place_z,
    )
    half = keep + swap(send, "c", 1)
    half = sum_four(half, "y", 1)
    half = half + swap(half, "z", 1)
    half = sum_four(half, "z", 2)
    parts = quad_merge(half, swap(half, "c", 1), diagonal, stack, True)

    pieces = [parts[0]] + [swap(parts[s], "x", s) for s in range(1, 4)]

    def place_x(n):
        return lax.axis_index("x") ^ n

    stack, diagonal, keep, send = quad_gram(
        pieces, [(piece, width) for piece in pieces], width, place_x
    )
    half = keep + swap(send, "c", 1)
    half = sum_four(half, "y", 1)
    half = half + swap(half, "z", 1)
    half = sum_four(half, "z", 2)
    half = sum_four(half, "x", 1)
    (merged,) = quad_merge(half, swap(half, "c", 1), diagonal, stack, False)
    return merged


def solution(mesh):
    split = Mesh(mesh.devices.reshape(4, 2, 4, 8), ("y", "c", "x", "z"))
    return jax.shard_map(
        body,
        mesh=split,
        in_specs=(P(("x", "z"), ("y", "c")),),
        out_specs=P(None, ("y", "c", "x", "z")),
        check_vma=False,
    )
```

```python
import jax
import jax.numpy as jnp
from jax import lax
from jax.experimental import pallas as pl
from jax.experimental.pallas import tpu as pltpu
from jax.sharding import Mesh
from jax.sharding import PartitionSpec as P

ITERS = 3
RANK = 64
ROWS_CONTRACT = (((1,), (1,)), ((), ()))
HIGHEST = lax.Precision.HIGHEST
F32 = jnp.float32
BF16 = jnp.bfloat16


def call(kernel, name, shapes, *operands, scratch=(), anywhere=False, waits=()):
    spec = pl.BlockSpec(memory_space=pl.ANY if anywhere else pltpu.VMEM)
    source = pl.BlockSpec(memory_space=pltpu.HBM) if anywhere else spec
    passing = [pl.BlockSpec(memory_space=pl.ANY)] * len(waits)
    ins, outs, passed = len(operands), len(shapes), len(waits)

    def run(*refs):
        kernel(*refs[:ins], *refs[ins + passed : ins + passed + outs], *refs[ins + 2 * passed + outs :])

    return pl.pallas_call(
        run,
        out_shape=[jax.ShapeDtypeStruct(shape, F32) for shape in shapes]
        + [jax.ShapeDtypeStruct(wait.shape, F32) for wait in waits],
        in_specs=[source] * ins + passing,
        out_specs=[spec] * outs + passing,
        input_output_aliases={ins + n: outs + n for n in range(passed)},
        scratch_shapes=list(scratch),
        compiler_params=pltpu.CompilerParams(vmem_limit_bytes=40 * 1024 * 1024),
        name=name,
    )(*operands, *waits)


def exact(left, right):
    return jnp.dot(left, right, precision=HIGHEST, preferred_element_type=F32)


def exact_rows(left, right):
    return lax.dot_general(
        left, right, ROWS_CONTRACT, precision=HIGHEST, preferred_element_type=F32
    )


def part(value):
    high = value.astype(BF16)
    return high, value - high.astype(F32)


def product(left, right):
    left_high, left_rest = part(left)
    right_high, right_rest = part(right)

    def dot(a, b):
        return jnp.dot(a, b, preferred_element_type=F32)

    return dot(left_high, right_high) + (
        dot(left_high, right_rest.astype(BF16)) + dot(left_rest.astype(BF16), right_high)
    )


def gram_terms(rows):
    high, rest = part(rows)
    middle, rest = part(rest)
    low = rest.astype(BF16)

    def dot(a, b):
        return lax.dot_general(a, b, ROWS_CONTRACT, preferred_element_type=F32)

    return dot(high, high) + dot(middle, middle), dot(high, middle) + dot(high, low)


def splat_lane(block, lane):
    return jnp.broadcast_to(block[:, lane : lane + 1], (8, 128))


def splat_row(block, row):
    return jnp.broadcast_to(block[row : row + 1, :], (8, 128))


def orthonormal(images):
    rank = images[0].shape[0]
    blocks = rank // 8
    row = lax.broadcasted_iota(jnp.int32, (8, 128), 0)
    pad = jnp.zeros((128 - rank, 128), F32)
    inner = [exact_rows(image, jnp.concatenate([image, pad], 0)) for image in images]
    inners = [[s[8 * i : 8 * i + 8] for i in range(blocks)] for s in inner]
    targets = [[z[8 * i : 8 * i + 8] for i in range(blocks)] for z in images]
    results = [[None] * blocks for _ in images]
    ahead = [None] * len(images)
    for k in range(blocks):
        last = k == blocks - 1
        columns = []
        for n, s in enumerate(inners):
            found = {i: [splat_lane(s[i], 8 * k + j) for j in range(8)] for i in range(k + 1, blocks)}
            if ahead[n] is None:
                ahead[n] = [splat_lane(s[k], 8 * k + j) for j in range(8)]
            found[k] = ahead[n]
            columns.append(found)
        if not last:
            ahead = [[splat_lane(s[k + 1], 8 * k + 8 + j) for j in range(8)] for s in inners]
        pivots = [jnp.ones((8, 128), F32) for _ in images]
        for j in range(8):
            for n in range(len(images)):
                s, z, c = inners[n], targets[n], columns[n]
                pivot = splat_row(c[k][j], j)
                inverse = 1.0 / pivot
                pivots[n] = jnp.where(row == j, pivot, pivots[n])
                row_s = None if last else splat_row(s[k], j) * inverse
                row_z = splat_row(z[k], j) * inverse
                row_c = [splat_row(c[k][m], j) * inverse if m > j else None for m in range(8)]
                for i in range(k, blocks):
                    if i == k and j == 7:
                        continue
                    weight = jnp.where(row > j, c[i][j], 0.0) if i == k else c[i][j]
                    if not last:
                        s[i] = s[i] - weight * row_s
                    z[i] = z[i] - weight * row_z
                    for m in range(j + 1, 8):
                        c[i][m] = c[i][m] - weight * row_c[m]
                if not last:
                    weight = c[k + 1][j] * inverse
                    for m in range(8):
                        ahead[n][m] = ahead[n][m] - weight * splat_row(c[k + 1][j], m)
        for n in range(len(images)):
            results[n][k] = targets[n][k] * lax.rsqrt(pivots[n])
    return [jnp.concatenate(result, 0) for result in results]


def bases(grams):
    first = tuple(orthonormal([gram[:RANK] for gram in grams]))

    def step(_, found):
        return tuple(orthonormal([exact(x, gram) for x, gram in zip(found, grams)]))

    return lax.fori_loop(0, ITERS - 1, step, first)


def two_levels(gram):
    pair = 2 * RANK
    left, right = bases([gram[:pair, :pair], gram[pair:, pair:]])
    cross = exact_rows(exact(left, gram[:pair, pair:]), right)
    upper = exact_rows(exact(left, gram[:pair, :pair]), left)
    lower = exact_rows(exact(right, gram[pair:, pair:]), right)
    both = jnp.concatenate(
        [jnp.concatenate([upper, cross], 1), jnp.concatenate([cross.T, lower], 1)], 0
    )
    (top,) = bases([both])
    weights = jnp.concatenate([exact(top[:, :RANK], left), exact(top[:, RANK:], right)], 1)
    return weights, exact_rows(exact(top, both), top)


def signs():
    where = lax.axis_index("z")
    odd = lax.rem(where, 2)
    return where, odd, 2 * odd - 1


def pack(factor, mine, width, groups):
    count = sum(len(group) for group in groups)

    def kernel(source, *refs):
        targets, sems = refs[:-1], refs[-1]
        where, odd, sign = signs()
        first = where if mine else where + 1 - 2 * odd
        step = sign if mine else -sign
        copies = []
        for target, group in zip(targets, groups):
            for at, d in enumerate(group):
                chunk = lax.rem(first + step * d + 8, 8)
                for x in range(4):
                    start = pl.multiple_of((x * 8 + chunk) * width, width)
                    copies.append(
                        pltpu.make_async_copy(
                            source.at[:, pl.ds(start, width)],
                            target.at[at, :, pl.ds(x * width, width)],
                            sems.at[len(copies)],
                        )
                    )
        for copy in copies:
            copy.start()
        for copy in copies:
            copy.wait()

    return call(
        kernel,
        "pack",
        [(len(group), RANK, 4 * width) for group in groups],
        factor,
        scratch=[pltpu.SemaphoreType.DMA((4 * count,))],
        anywhere=True,
    )


def after(block, arrival):
    def kernel():
        pass

    return call(kernel, "after", [], waits=(block, arrival))


def pair_terms(own, other):
    symmetric = half = None
    for a, b in zip(own, other):
        terms = gram_terms(jnp.concatenate([a, b], 0))
        symmetric = terms[0] if symmetric is None else symmetric + terms[0]
        half = terms[1] if half is None else half + terms[1]
    return symmetric, half


def near_gram(own, other):
    def kernel(one, two, other_ref, out_ref):
        symmetric, half = pair_terms([one[0], two[0]], [other_ref[0], other_ref[1]])
        out_ref[:, : 2 * RANK] = symmetric
        out_ref[:, 2 * RANK :] = half

    (terms,) = call(kernel, "near_gram", [(2 * RANK, 4 * RANK)], *own, other)
    return terms


def pair_gram(near, own, other, waits):
    def kernel(near_ref, own_none, own_far, other_none, other_far, out_ref):
        symmetric, half = pair_terms(
            [own_none[0], own_far[0]], [other_none[0], other_far[0]]
        )
        half = half + near_ref[:, 2 * RANK :]
        gram = (symmetric + near_ref[:, : 2 * RANK]) + (half + half.T)
        out_ref[:, : 2 * RANK] = gram[:RANK]
        out_ref[:, 2 * RANK :] = gram[RANK:, RANK:]

    return call(kernel, "pair_gram", [(RANK, 3 * RANK)], near, *own, *other, waits=waits)


def pair_solve(here, there, own, other, waits):
    width = own.shape[2]

    def kernel(here_ref, there_ref, own_ref, other_ref, basis_ref, merged_ref):
        where, odd, sign = signs()
        upper = odd == 1
        here = here_ref[...]
        there = there_ref[...]
        own_own = here[:, :RANK] + there[:, 2 * RANK :]
        cross = here[:, RANK : 2 * RANK] + there[:, RANK : 2 * RANK].T
        other_other = here[:, 2 * RANK :] + there[:, :RANK]
        top = jnp.where(upper, other_other, own_own)
        bottom = jnp.where(upper, own_own, other_other)
        cross = jnp.where(upper, cross.T, cross)
        gram = jnp.concatenate(
            [jnp.concatenate([top, cross], 1), jnp.concatenate([cross.T, bottom], 1)], 0
        )
        (basis,) = bases([gram])
        merged_gram = exact_rows(exact(basis, gram), basis)
        swapped = jnp.concatenate([basis[:, RANK:], basis[:, :RANK]], 1)
        weights = jnp.where(upper, swapped, basis)
        basis_ref[:, : 2 * RANK] = weights
        basis_ref[:, 2 * RANK :] = merged_gram
        rows = jnp.concatenate([own_ref[0], other_ref[0]], 0)
        merged_ref[:, :width] = product(weights, rows)
        merged_ref[:, width : width + RANK] = merged_gram
        merged_ref[:, width + RANK :] = jnp.zeros((RANK, RANK), F32)

    shapes = [(RANK, 3 * RANK), (RANK, width + 2 * RANK)]
    return call(kernel, "pair_solve", shapes, here, there, own, other, waits=waits)


def near_merge(weights, own, other):
    width = own[0].shape[2]

    def kernel(*refs):
        for n in range(3):
            rows = jnp.concatenate([refs[3 + n][0], refs[6 + n][0]], 0)
            refs[9 + n][...] = product(refs[n][:, : 2 * RANK], rows)

    return call(kernel, "near_merge", [(RANK, width)] * 3, *weights, *own, *other)


def quad_gram(pieces, grams, width, place):
    half = RANK // 2

    def kernel(*refs):
        ins, diagonals, (stack, diagonal, keep, send, packed) = refs[:4], refs[4:8], refs[8:]
        for n in range(4):
            start = pl.multiple_of(place(n) * RANK, RANK)
            stack[pl.ds(start, RANK), :] = ins[n][:, :width]
            lane = grams[n][1]
            diagonal[pl.ds(start, RANK), :] = diagonals[n][:, lane : lane + RANK]
        symmetric, terms = gram_terms(stack[...])
        gram = symmetric + (terms + terms.T)
        at = 0
        for i in range(3):
            columns = (3 - i) * RANK
            packed[:, at : at + columns] = gram[i * RANK : (i + 1) * RANK, (i + 1) * RANK :]
            at += columns
        core = lax.axis_index("c")
        keep[...] = packed[pl.ds(pl.multiple_of(core * half, half), half), :]
        send[...] = packed[pl.ds(pl.multiple_of((1 - core) * half, half), half), :]

    return call(
        kernel,
        "quad_gram",
        [(4 * RANK, width), (4 * RANK, RANK), (half, 6 * RANK), (half, 6 * RANK)],
        *pieces,
        *(gram for gram, _ in grams),
        scratch=[pltpu.VMEM((RANK, 6 * RANK), F32)],
    )


def quad_merge(own_half, other_half, diagonal, stack, split):
    rows, width = stack.shape
    share = width // 4 if split else width

    def kernel(own_ref, other_ref, diagonal_ref, stack_ref, *outs):
        core = lax.axis_index("c")
        first = core == 0
        own_half = own_ref[...]
        other_half = other_ref[...]
        packed = jnp.concatenate(
            [
                jnp.where(first, own_half, other_half),
                jnp.where(first, other_half, own_half),
            ],
            0,
        )
        at = 0
        found = {}
        for i in range(4):
            found[i, i] = diagonal_ref[i * RANK : (i + 1) * RANK, :]
            for j in range(i + 1, 4):
                found[i, j] = packed[:, at : at + RANK]
                found[j, i] = found[i, j].T
                at += RANK
        gram = jnp.concatenate(
            [jnp.concatenate([found[i, j] for j in range(4)], 1) for i in range(4)], 0
        )
        weights, merged_gram = two_levels(gram)
        if not split:
            outs[0][...] = product(weights, stack_ref[...])
            return
        x = lax.axis_index("x")
        for s in range(4):
            start = pl.multiple_of((x ^ s) * share, share)
            outs[s][:, :share] = product(weights, stack_ref[:, pl.ds(start, share)])
            outs[s][:, share : share + RANK] = merged_gram
            outs[s][:, share + RANK :] = jnp.zeros((RANK, RANK), F32)

    shapes = [(RANK, share + 2 * RANK)] * 4 if split else [(RANK, share)]
    return call(kernel, "quad_merge", shapes, own_half, other_half, diagonal, stack)


def swap(block, axis, bits):
    count = lax.axis_size(axis)
    return lax.ppermute(block, axis, [(i, i ^ bits) for i in range(count)])


def outward(block, distance):
    route = [(i, (i + (distance if i % 2 else -distance)) % 8) for i in range(8)]
    return lax.ppermute(block, "z", route)


def sum_four(block, axis, unit):
    one, two, three = (swap(block, axis, unit * s) for s in (1, 2, 3))
    return (block + one) + (two + three)


def body(factor):
    width = factor.shape[1] // 32
    factor = pltpu.with_memory_space_constraint(factor, pltpu.HBM)
    near, far, none = pack(factor, False, width, [(1, 2), (3,), (0,)])
    other_near = swap(near, "z", 1)
    other_far = swap(far, "z", 1)
    none, other_far = after(none, other_far)
    other_none = swap(none, "z", 1)
    own_one, own_two, own_none, own_far = pack(factor, True, width, [(1,), (2,), (0,), (3,)])
    first_own = outward(own_one, 1)
    relay_own = outward(own_two, 1)
    from_near = outward(other_near, 1)

    gram, first_own, relay_own = pair_gram(
        near_gram([own_one, own_two], other_near),
        [own_none, own_far],
        [other_none, other_far],
        [first_own, relay_own],
    )
    second_own = swap(relay_own, "z", 1)
    gram = gram + swap(gram, "c", 1)
    gram = sum_four(gram, "y", 1)
    basis, far, from_near, second_own = pair_solve(
        gram, swap(gram, "z", 1), own_far, other_far, [from_near, second_own]
    )
    second_other = swap(from_near[1:], "z", 1)
    basis_one = outward(basis, 1)
    basis_two = outward(basis, 2)
    far = outward(far, 3)
    pieces = near_merge(
        [basis, basis_one, basis_two],
        [own_none, first_own, second_own],
        [other_none, from_near, second_other],
    )

    def place_z(n):
        where, odd, sign = signs()
        offset = (0, 1, -1, 2)[n]
        return lax.rem(lax.div(where, 2) + sign * offset + 8, 4)

    reach = 4 * width
    lane = 2 * RANK
    stack, diagonal, keep, send = quad_gram(
        [*pieces, far],
        [(basis, lane), (basis_one, lane), (basis_two, lane), (far, reach)],
        reach,
        place_z,
    )
    half = keep + swap(send, "c", 1)
    half = sum_four(half, "y", 1)
    half = half + swap(half, "z", 1)
    half = sum_four(half, "z", 2)
    parts = quad_merge(half, swap(half, "c", 1), diagonal, stack, True)

    pieces = [parts[0]] + [swap(parts[s], "x", s) for s in range(1, 4)]

    def place_x(n):
        return lax.axis_index("x") ^ n

    stack, diagonal, keep, send = quad_gram(
        pieces, [(piece, width) for piece in pieces], width, place_x
    )
    half = keep + swap(send, "c", 1)
    half = sum_four(half, "y", 1)
    half = half + swap(half, "z", 1)
    half = sum_four(half, "z", 2)
    half = sum_four(half, "x", 1)
    (merged,) = quad_merge(half, swap(half, "c", 1), diagonal, stack, False)
    return merged


def solution(mesh):
    split = Mesh(mesh.devices.reshape(4, 2, 4, 8), ("y", "c", "x", "z"))
    return jax.shard_map(
        body,
        mesh=split,
        in_specs=(P(("x", "z"), ("y", "c")),),
        out_specs=P(None, ("y", "c", "x", "z")),
        check_vma=False,
    )
```

```python
import jax
import jax.numpy as jnp
from jax import lax
from jax.experimental import pallas as pl
from jax.experimental.pallas import tpu as pltpu
from jax.sharding import Mesh
from jax.sharding import PartitionSpec as P

ITERS = 3
RANK = 64
ROWS_CONTRACT = (((1,), (1,)), ((), ()))
HIGHEST = lax.Precision.HIGHEST
F32 = jnp.float32
BF16 = jnp.bfloat16


def call(kernel, name, shapes, *operands, scratch=(), anywhere=False, waits=()):
    spec = pl.BlockSpec(memory_space=pl.ANY if anywhere else pltpu.VMEM)
    source = pl.BlockSpec(memory_space=pltpu.HBM) if anywhere else spec
    passing = [pl.BlockSpec(memory_space=pl.ANY)] * len(waits)
    ins, outs, passed = len(operands), len(shapes), len(waits)

    def run(*refs):
        kernel(*refs[:ins], *refs[ins + passed : ins + passed + outs], *refs[ins + 2 * passed + outs :])

    return pl.pallas_call(
        run,
        out_shape=[jax.ShapeDtypeStruct(shape, F32) for shape in shapes]
        + [jax.ShapeDtypeStruct(wait.shape, F32) for wait in waits],
        in_specs=[source] * ins + passing,
        out_specs=[spec] * outs + passing,
        input_output_aliases={ins + n: outs + n for n in range(passed)},
        scratch_shapes=list(scratch),
        compiler_params=pltpu.CompilerParams(vmem_limit_bytes=40 * 1024 * 1024),
        name=name,
    )(*operands, *waits)


def exact(left, right):
    return jnp.dot(left, right, precision=HIGHEST, preferred_element_type=F32)


def exact_rows(left, right):
    return lax.dot_general(
        left, right, ROWS_CONTRACT, precision=HIGHEST, preferred_element_type=F32
    )


def part(value):
    high = value.astype(BF16)
    return high, value - high.astype(F32)


def product(left, right):
    left_high, left_rest = part(left)
    right_high, right_rest = part(right)

    def dot(a, b):
        return jnp.dot(a, b, preferred_element_type=F32)

    return dot(left_high, right_high) + (
        dot(left_high, right_rest.astype(BF16)) + dot(left_rest.astype(BF16), right_high)
    )


def gram_terms(rows):
    high, rest = part(rows)
    middle, rest = part(rest)
    low = rest.astype(BF16)

    def dot(a, b):
        return lax.dot_general(a, b, ROWS_CONTRACT, preferred_element_type=F32)

    return dot(high, high) + dot(middle, middle), dot(high, middle) + dot(high, low)


def splat_lane(block, lane):
    return jnp.take_along_axis(block, jnp.full((8, 128), lane, jnp.int32), axis=1)


def splat_row(block, row):
    return jnp.broadcast_to(block[row : row + 1, :], (8, 128))


def orthonormal(images):
    rank = images[0].shape[0]
    blocks = rank // 8
    row = lax.broadcasted_iota(jnp.int32, (8, 128), 0)
    pad = jnp.zeros((128 - rank, 128), F32)
    inner = [exact_rows(image, jnp.concatenate([image, pad], 0)) for image in images]
    inners = [[s[8 * i : 8 * i + 8] for i in range(blocks)] for s in inner]
    targets = [[z[8 * i : 8 * i + 8] for i in range(blocks)] for z in images]
    results = [[None] * blocks for _ in images]
    ahead = [None] * len(images)
    for k in range(blocks):
        last = k == blocks - 1
        columns = []
        for n, s in enumerate(inners):
            found = {i: [splat_lane(s[i], 8 * k + j) for j in range(8)] for i in range(k + 1, blocks)}
            if ahead[n] is None:
                ahead[n] = [splat_lane(s[k], 8 * k + j) for j in range(8)]
            found[k] = ahead[n]
            columns.append(found)
        if not last:
            ahead = [[splat_lane(s[k + 1], 8 * k + 8 + j) for j in range(8)] for s in inners]
        pivots = [jnp.ones((8, 128), F32) for _ in images]
        for j in range(8):
            for n in range(len(images)):
                s, z, c = inners[n], targets[n], columns[n]
                pivot = splat_row(c[k][j], j)
                inverse = 1.0 / pivot
                pivots[n] = jnp.where(row == j, pivot, pivots[n])
                row_s = None if last else splat_row(s[k], j) * inverse
                row_z = splat_row(z[k], j) * inverse
                row_c = [splat_row(c[k][m], j) * inverse if m > j else None for m in range(8)]
                for i in range(k, blocks):
                    if i == k and j == 7:
                        continue
                    weight = jnp.where(row > j, c[i][j], 0.0) if i == k else c[i][j]
                    if not last:
                        s[i] = s[i] - weight * row_s
                    z[i] = z[i] - weight * row_z
                    for m in range(j + 1, 8):
                        c[i][m] = c[i][m] - weight * row_c[m]
                if not last:
                    weight = c[k + 1][j] * inverse
                    for m in range(8):
                        ahead[n][m] = ahead[n][m] - weight * splat_row(c[k + 1][j], m)
        for n in range(len(images)):
            results[n][k] = targets[n][k] * lax.rsqrt(pivots[n])
    return [jnp.concatenate(result, 0) for result in results]


def bases(grams):
    first = tuple(orthonormal([gram[:RANK] for gram in grams]))

    def step(_, found):
        return tuple(orthonormal([exact(x, gram) for x, gram in zip(found, grams)]))

    return lax.fori_loop(0, ITERS - 1, step, first)


def two_levels(gram):
    pair = 2 * RANK
    left, right = bases([gram[:pair, :pair], gram[pair:, pair:]])
    cross = exact_rows(exact(left, gram[:pair, pair:]), right)
    upper = exact_rows(exact(left, gram[:pair, :pair]), left)
    lower = exact_rows(exact(right, gram[pair:, pair:]), right)
    both = jnp.concatenate(
        [jnp.concatenate([upper, cross], 1), jnp.concatenate([cross.T, lower], 1)], 0
    )
    (top,) = bases([both])
    weights = jnp.concatenate([exact(top[:, :RANK], left), exact(top[:, RANK:], right)], 1)
    return weights, exact_rows(exact(top, both), top)


def signs():
    where = lax.axis_index("z")
    odd = lax.rem(where, 2)
    return where, odd, 2 * odd - 1


def pack(factor, mine, width, groups):
    count = sum(len(group) for group in groups)

    def kernel(source, *refs):
        targets, sems = refs[:-1], refs[-1]
        where, odd, sign = signs()
        first = where if mine else where + 1 - 2 * odd
        step = sign if mine else -sign
        copies = []
        for target, group in zip(targets, groups):
            for at, d in enumerate(group):
                chunk = lax.rem(first + step * d + 8, 8)
                for x in range(4):
                    start = pl.multiple_of((x * 8 + chunk) * width, width)
                    copies.append(
                        pltpu.make_async_copy(
                            source.at[:, pl.ds(start, width)],
                            target.at[at, :, pl.ds(x * width, width)],
                            sems.at[len(copies)],
                        )
                    )
        for copy in copies:
            copy.start()
        for copy in copies:
            copy.wait()

    return call(
        kernel,
        "pack",
        [(len(group), RANK, 4 * width) for group in groups],
        factor,
        scratch=[pltpu.SemaphoreType.DMA((4 * count,))],
        anywhere=True,
    )


def after(block, arrival):
    def kernel():
        pass

    return call(kernel, "after", [], waits=(block, arrival))


def pair_terms(own, other):
    symmetric = half = None
    for a, b in zip(own, other):
        terms = gram_terms(jnp.concatenate([a, b], 0))
        symmetric = terms[0] if symmetric is None else symmetric + terms[0]
        half = terms[1] if half is None else half + terms[1]
    return symmetric, half


def near_gram(own, other):
    def kernel(one, two, other_ref, out_ref):
        symmetric, half = pair_terms([one[0], two[0]], [other_ref[0], other_ref[1]])
        out_ref[:, : 2 * RANK] = symmetric
        out_ref[:, 2 * RANK :] = half

    (terms,) = call(kernel, "near_gram", [(2 * RANK, 4 * RANK)], *own, other)
    return terms


def pair_gram(near, own, other, waits):
    def kernel(near_ref, own_none, own_far, other_none, other_far, out_ref):
        symmetric, half = pair_terms(
            [own_none[0], own_far[0]], [other_none[0], other_far[0]]
        )
        half = half + near_ref[:, 2 * RANK :]
        gram = (symmetric + near_ref[:, : 2 * RANK]) + (half + half.T)
        out_ref[:, : 2 * RANK] = gram[:RANK]
        out_ref[:, 2 * RANK :] = gram[RANK:, RANK:]

    return call(kernel, "pair_gram", [(RANK, 3 * RANK)], near, *own, *other, waits=waits)


def pair_solve(here, there, own, other, waits):
    width = own.shape[2]

    def kernel(here_ref, there_ref, own_ref, other_ref, basis_ref, merged_ref):
        where, odd, sign = signs()
        upper = odd == 1
        here = here_ref[...]
        there = there_ref[...]
        own_own = here[:, :RANK] + there[:, 2 * RANK :]
        cross = here[:, RANK : 2 * RANK] + there[:, RANK : 2 * RANK].T
        other_other = here[:, 2 * RANK :] + there[:, :RANK]
        top = jnp.where(upper, other_other, own_own)
        bottom = jnp.where(upper, own_own, other_other)
        cross = jnp.where(upper, cross.T, cross)
        gram = jnp.concatenate(
            [jnp.concatenate([top, cross], 1), jnp.concatenate([cross.T, bottom], 1)], 0
        )
        (basis,) = bases([gram])
        merged_gram = exact_rows(exact(basis, gram), basis)
        swapped = jnp.concatenate([basis[:, RANK:], basis[:, :RANK]], 1)
        weights = jnp.where(upper, swapped, basis)
        basis_ref[:, : 2 * RANK] = weights
        basis_ref[:, 2 * RANK :] = merged_gram
        rows = jnp.concatenate([own_ref[0], other_ref[0]], 0)
        merged_ref[:, :width] = product(weights, rows)
        merged_ref[:, width : width + RANK] = merged_gram
        merged_ref[:, width + RANK :] = jnp.zeros((RANK, RANK), F32)

    shapes = [(RANK, 3 * RANK), (RANK, width + 2 * RANK)]
    return call(kernel, "pair_solve", shapes, here, there, own, other, waits=waits)


def near_merge(weights, own, other):
    width = own[0].shape[2]

    def kernel(*refs):
        for n in range(3):
            rows = jnp.concatenate([refs[3 + n][0], refs[6 + n][0]], 0)
            refs[9 + n][...] = product(refs[n][:, : 2 * RANK], rows)

    return call(kernel, "near_merge", [(RANK, width)] * 3, *weights, *own, *other)


def quad_gram(pieces, grams, width, place):
    half = RANK // 2

    def kernel(*refs):
        ins, diagonals, (stack, diagonal, keep, send, packed) = refs[:4], refs[4:8], refs[8:]
        for n in range(4):
            start = pl.multiple_of(place(n) * RANK, RANK)
            stack[pl.ds(start, RANK), :] = ins[n][:, :width]
            lane = grams[n][1]
            diagonal[pl.ds(start, RANK), :] = diagonals[n][:, lane : lane + RANK]
        symmetric, terms = gram_terms(stack[...])
        gram = symmetric + (terms + terms.T)
        at = 0
        for i in range(3):
            columns = (3 - i) * RANK
            packed[:, at : at + columns] = gram[i * RANK : (i + 1) * RANK, (i + 1) * RANK :]
            at += columns
        core = lax.axis_index("c")
        keep[...] = packed[pl.ds(pl.multiple_of(core * half, half), half), :]
        send[...] = packed[pl.ds(pl.multiple_of((1 - core) * half, half), half), :]

    return call(
        kernel,
        "quad_gram",
        [(4 * RANK, width), (4 * RANK, RANK), (half, 6 * RANK), (half, 6 * RANK)],
        *pieces,
        *(gram for gram, _ in grams),
        scratch=[pltpu.VMEM((RANK, 6 * RANK), F32)],
    )


def quad_merge(own_half, other_half, diagonal, stack, split):
    rows, width = stack.shape
    share = width // 4 if split else width

    def kernel(own_ref, other_ref, diagonal_ref, stack_ref, *outs):
        core = lax.axis_index("c")
        first = core == 0
        own_half = own_ref[...]
        other_half = other_ref[...]
        packed = jnp.concatenate(
            [
                jnp.where(first, own_half, other_half),
                jnp.where(first, other_half, own_half),
            ],
            0,
        )
        at = 0
        found = {}
        for i in range(4):
            found[i, i] = diagonal_ref[i * RANK : (i + 1) * RANK, :]
            for j in range(i + 1, 4):
                found[i, j] = packed[:, at : at + RANK]
                found[j, i] = found[i, j].T
                at += RANK
        gram = jnp.concatenate(
            [jnp.concatenate([found[i, j] for j in range(4)], 1) for i in range(4)], 0
        )
        weights, merged_gram = two_levels(gram)
        if not split:
            outs[0][...] = product(weights, stack_ref[...])
            return
        x = lax.axis_index("x")
        for s in range(4):
            start = pl.multiple_of((x ^ s) * share, share)
            outs[s][:, :share] = product(weights, stack_ref[:, pl.ds(start, share)])
            outs[s][:, share : share + RANK] = merged_gram
            outs[s][:, share + RANK :] = jnp.zeros((RANK, RANK), F32)

    shapes = [(RANK, share + 2 * RANK)] * 4 if split else [(RANK, share)]
    return call(kernel, "quad_merge", shapes, own_half, other_half, diagonal, stack)


def swap(block, axis, bits):
    count = lax.axis_size(axis)
    return lax.ppermute(block, axis, [(i, i ^ bits) for i in range(count)])


def outward(block, distance):
    route = [(i, (i + (distance if i % 2 else -distance)) % 8) for i in range(8)]
    return lax.ppermute(block, "z", route)


def sum_four(block, axis, unit):
    one, two, three = (swap(block, axis, unit * s) for s in (1, 2, 3))
    return (block + one) + (two + three)


def body(factor):
    width = factor.shape[1] // 32
    factor = pltpu.with_memory_space_constraint(factor, pltpu.HBM)
    near, far, none = pack(factor, False, width, [(1, 2), (3,), (0,)])
    other_near = swap(near, "z", 1)
    other_far = swap(far, "z", 1)
    none, other_far = after(none, other_far)
    other_none = swap(none, "z", 1)
    own_one, own_two, own_none, own_far = pack(factor, True, width, [(1,), (2,), (0,), (3,)])
    first_own = outward(own_one, 1)
    relay_own = outward(own_two, 1)
    from_near = outward(other_near, 1)

    gram, first_own, relay_own = pair_gram(
        near_gram([own_one, own_two], other_near),
        [own_none, own_far],
        [other_none, other_far],
        [first_own, relay_own],
    )
    second_own = swap(relay_own, "z", 1)
    gram = gram + swap(gram, "c", 1)
    gram = sum_four(gram, "y", 1)
    basis, far, from_near, second_own = pair_solve(
        gram, swap(gram, "z", 1), own_far, other_far, [from_near, second_own]
    )
    second_other = swap(from_near[1:], "z", 1)
    basis_one = outward(basis, 1)
    basis_two = outward(basis, 2)
    far = outward(far, 3)
    pieces = near_merge(
        [basis, basis_one, basis_two],
        [own_none, first_own, second_own],
        [other_none, from_near, second_other],
    )

    def place_z(n):
        where, odd, sign = signs()
        offset = (0, 1, -1, 2)[n]
        return lax.rem(lax.div(where, 2) + sign * offset + 8, 4)

    reach = 4 * width
    lane = 2 * RANK
    stack, diagonal, keep, send = quad_gram(
        [*pieces, far],
        [(basis, lane), (basis_one, lane), (basis_two, lane), (far, reach)],
        reach,
        place_z,
    )
    half = keep + swap(send, "c", 1)
    half = sum_four(half, "y", 1)
    half = half + swap(half, "z", 1)
    half = sum_four(half, "z", 2)
    parts = quad_merge(half, swap(half, "c", 1), diagonal, stack, True)

    pieces = [parts[0]] + [swap(parts[s], "x", s) for s in range(1, 4)]

    def place_x(n):
        return lax.axis_index("x") ^ n

    stack, diagonal, keep, send = quad_gram(
        pieces, [(piece, width) for piece in pieces], width, place_x
    )
    half = keep + swap(send, "c", 1)
    half = sum_four(half, "y", 1)
    half = half + swap(half, "z", 1)
    half = sum_four(half, "z", 2)
    half = sum_four(half, "x", 1)
    (merged,) = quad_merge(half, swap(half, "c", 1), diagonal, stack, False)
    return merged


def solution(mesh):
    split = Mesh(mesh.devices.reshape(4, 2, 4, 8), ("y", "c", "x", "z"))
    return jax.shard_map(
        body,
        mesh=split,
        in_specs=(P(("x", "z"), ("y", "c")),),
        out_specs=P(None, ("y", "c", "x", "z")),
        check_vma=False,
    )
```

```python
import jax
import jax.numpy as jnp
from jax import lax
from jax.experimental import pallas as pl
from jax.experimental.pallas import tpu as pltpu
from jax.sharding import Mesh
from jax.sharding import PartitionSpec as P

ITERS = 3
RANK = 64
ROWS_CONTRACT = (((1,), (1,)), ((), ()))
HIGHEST = lax.Precision.HIGHEST
F32 = jnp.float32
BF16 = jnp.bfloat16


def call(kernel, name, shapes, *operands, scratch=(), anywhere=False, waits=()):
    spec = pl.BlockSpec(memory_space=pl.ANY if anywhere else pltpu.VMEM)
    source = pl.BlockSpec(memory_space=pltpu.HBM) if anywhere else spec
    passing = [pl.BlockSpec(memory_space=pl.ANY)] * len(waits)
    ins, outs, passed = len(operands), len(shapes), len(waits)

    def run(*refs):
        kernel(*refs[:ins], *refs[ins + passed : ins + passed + outs], *refs[ins + 2 * passed + outs :])

    return pl.pallas_call(
        run,
        out_shape=[jax.ShapeDtypeStruct(shape, F32) for shape in shapes]
        + [jax.ShapeDtypeStruct(wait.shape, F32) for wait in waits],
        in_specs=[source] * ins + passing,
        out_specs=[spec] * outs + passing,
        input_output_aliases={ins + n: outs + n for n in range(passed)},
        scratch_shapes=list(scratch),
        compiler_params=pltpu.CompilerParams(vmem_limit_bytes=40 * 1024 * 1024),
        name=name,
    )(*operands, *waits)


def exact(left, right):
    return jnp.dot(left, right, precision=HIGHEST, preferred_element_type=F32)


def exact_rows(left, right):
    return lax.dot_general(
        left, right, ROWS_CONTRACT, precision=HIGHEST, preferred_element_type=F32
    )


def part(value):
    high = value.astype(BF16)
    return high, value - high.astype(F32)


def product(left, right):
    left_high, left_rest = part(left)
    right_high, right_rest = part(right)

    def dot(a, b):
        return jnp.dot(a, b, preferred_element_type=F32)

    return dot(left_high, right_high) + (
        dot(left_high, right_rest.astype(BF16)) + dot(left_rest.astype(BF16), right_high)
    )


def gram_terms(rows):
    high, rest = part(rows)
    middle, rest = part(rest)
    low = rest.astype(BF16)

    def dot(a, b):
        return lax.dot_general(a, b, ROWS_CONTRACT, preferred_element_type=F32)

    return dot(high, high) + dot(middle, middle), dot(high, middle) + dot(high, low)


def splat_lane(block, lane):
    return jnp.take_along_axis(block, jnp.full((8, 128), lane, jnp.int32), axis=1)


def splat_row(block, row):
    return jnp.broadcast_to(block[row : row + 1, :], (8, 128))


def orthonormal(images):
    rank = images[0].shape[0]
    blocks = rank // 8
    row = lax.broadcasted_iota(jnp.int32, (8, 128), 0)
    pad = jnp.zeros((128 - rank, 128), F32)
    inner = [exact_rows(image, jnp.concatenate([image, pad], 0)) for image in images]
    inners = [[s[8 * i : 8 * i + 8] for i in range(blocks)] for s in inner]
    targets = [[z[8 * i : 8 * i + 8] for i in range(blocks)] for z in images]
    results = [[None] * blocks for _ in images]
    ahead = [None] * len(images)
    for k in range(blocks):
        last = k == blocks - 1
        columns = []
        for n, s in enumerate(inners):
            found = {i: [splat_lane(s[i], 8 * k + j) for j in range(8)] for i in range(k + 1, blocks)}
            if ahead[n] is None:
                ahead[n] = [splat_lane(s[k], 8 * k + j) for j in range(8)]
            found[k] = ahead[n]
            columns.append(found)
        if not last:
            ahead = [[splat_lane(s[k + 1], 8 * k + 8 + j) for j in range(8)] for s in inners]
        pivots = [jnp.ones((8, 128), F32) for _ in images]
        for j in range(8):
            for n in range(len(images)):
                s, z, c = inners[n], targets[n], columns[n]
                pivot = splat_row(c[k][j], j)
                inverse = 1.0 / pivot
                pivots[n] = jnp.where(row == j, pivot, pivots[n])
                row_s = None if last else splat_row(s[k], j) * inverse
                row_z = splat_row(z[k], j) * inverse
                row_c = [splat_row(c[k][m], j) * inverse if m > j else None for m in range(8)]
                for i in range(k, blocks):
                    if i == k and j == 7:
                        continue
                    weight = jnp.where(row > j, c[i][j], 0.0) if i == k else c[i][j]
                    if not last:
                        s[i] = s[i] - weight * row_s
                    z[i] = z[i] - weight * row_z
                    for m in range(j + 1, 8):
                        c[i][m] = c[i][m] - weight * row_c[m]
                if not last:
                    weight = c[k + 1][j] * inverse
                    for m in range(8):
                        ahead[n][m] = ahead[n][m] - weight * splat_row(c[k + 1][j], m)
        for n in range(len(images)):
            results[n][k] = targets[n][k] * lax.rsqrt(pivots[n])
    return [jnp.concatenate(result, 0) for result in results]


def bases(grams):
    first = tuple(orthonormal([gram[:RANK] for gram in grams]))

    def step(_, found):
        return tuple(orthonormal([exact(x, gram) for x, gram in zip(found, grams)]))

    return lax.fori_loop(0, ITERS - 1, step, first)


def two_levels(gram):
    pair = 2 * RANK
    left, right = bases([gram[:pair, :pair], gram[pair:, pair:]])
    cross = exact_rows(exact(left, gram[:pair, pair:]), right)
    upper = exact_rows(exact(left, gram[:pair, :pair]), left)
    lower = exact_rows(exact(right, gram[pair:, pair:]), right)
    both = jnp.concatenate(
        [jnp.concatenate([upper, cross], 1), jnp.concatenate([cross.T, lower], 1)], 0
    )
    (top,) = bases([both])
    weights = jnp.concatenate([exact(top[:, :RANK], left), exact(top[:, RANK:], right)], 1)
    return weights, exact_rows(exact(top, both), top)


def signs():
    where = lax.axis_index("z")
    odd = lax.rem(where, 2)
    return where, odd, 2 * odd - 1


def pack(factor, mine, width, groups):
    count = sum(len(group) for group in groups)

    def kernel(source, *refs):
        targets, sems = refs[:-1], refs[-1]
        where, odd, sign = signs()
        first = where if mine else where + 1 - 2 * odd
        step = sign if mine else -sign
        copies = []
        for target, group in zip(targets, groups):
            for at, d in enumerate(group):
                chunk = lax.rem(first + step * d + 8, 8)
                for x in range(4):
                    start = pl.multiple_of((x * 8 + chunk) * width, width)
                    copies.append(
                        pltpu.make_async_copy(
                            source.at[:, pl.ds(start, width)],
                            target.at[at, :, pl.ds(x * width, width)],
                            sems.at[len(copies)],
                        )
                    )
        for copy in copies:
            copy.start()
        for copy in copies:
            copy.wait()

    return call(
        kernel,
        "pack",
        [(len(group), RANK, 4 * width) for group in groups],
        factor,
        scratch=[pltpu.SemaphoreType.DMA((4 * count,))],
        anywhere=True,
    )


def after(block, arrival):
    def kernel():
        pass

    return call(kernel, "after", [], waits=(block, arrival))


def pair_terms(own, other):
    symmetric = half = None
    for a, b in zip(own, other):
        terms = gram_terms(jnp.concatenate([a, b], 0))
        symmetric = terms[0] if symmetric is None else symmetric + terms[0]
        half = terms[1] if half is None else half + terms[1]
    return symmetric, half


def near_gram(own, other):
    def kernel(one, two, other_ref, out_ref):
        symmetric, half = pair_terms([one[0], two[0]], [other_ref[0], other_ref[1]])
        out_ref[:, : 2 * RANK] = symmetric
        out_ref[:, 2 * RANK :] = half

    (terms,) = call(kernel, "near_gram", [(2 * RANK, 4 * RANK)], *own, other)
    return terms


def pair_gram(near, own, other, waits):
    def kernel(near_ref, own_none, own_far, other_none, other_far, out_ref):
        symmetric, half = pair_terms(
            [own_none[0], own_far[0]], [other_none[0], other_far[0]]
        )
        half = half + near_ref[:, 2 * RANK :]
        gram = (symmetric + near_ref[:, : 2 * RANK]) + (half + half.T)
        out_ref[:, : 2 * RANK] = gram[:RANK]
        out_ref[:, 2 * RANK :] = gram[RANK:, RANK:]

    return call(kernel, "pair_gram", [(RANK, 3 * RANK)], near, *own, *other, waits=waits)


def pair_solve(here, there, own, other, waits):
    width = own.shape[2]

    def kernel(here_ref, there_ref, own_ref, other_ref, basis_ref, merged_ref):
        where, odd, sign = signs()
        upper = odd == 1
        here = here_ref[...]
        there = there_ref[...]
        own_own = here[:, :RANK] + there[:, 2 * RANK :]
        cross = here[:, RANK : 2 * RANK] + there[:, RANK : 2 * RANK].T
        other_other = here[:, 2 * RANK :] + there[:, :RANK]
        top = jnp.where(upper, other_other, own_own)
        bottom = jnp.where(upper, own_own, other_other)
        cross = jnp.where(upper, cross.T, cross)
        gram = jnp.concatenate(
            [jnp.concatenate([top, cross], 1), jnp.concatenate([cross.T, bottom], 1)], 0
        )
        (basis,) = bases([gram])
        merged_gram = exact_rows(exact(basis, gram), basis)
        swapped = jnp.concatenate([basis[:, RANK:], basis[:, :RANK]], 1)
        weights = jnp.where(upper, swapped, basis)
        basis_ref[:, : 2 * RANK] = weights
        basis_ref[:, 2 * RANK :] = merged_gram
        rows = jnp.concatenate([own_ref[0], other_ref[0]], 0)
        merged_ref[:, :width] = product(weights, rows)
        merged_ref[:, width : width + RANK] = merged_gram
        merged_ref[:, width + RANK :] = jnp.zeros((RANK, RANK), F32)

    shapes = [(RANK, 3 * RANK), (RANK, width + 2 * RANK)]
    return call(kernel, "pair_solve", shapes, here, there, own, other, waits=waits)


def near_merge(weights, own, other):
    width = own[0].shape[2]

    def kernel(*refs):
        for n in range(3):
            rows = jnp.concatenate([refs[3 + n][0], refs[6 + n][0]], 0)
            refs[9 + n][...] = product(refs[n][:, : 2 * RANK], rows)

    return call(kernel, "near_merge", [(RANK, width)] * 3, *weights, *own, *other)


def quad_gram(pieces, grams, width, place):
    half = RANK // 2

    def kernel(*refs):
        ins, diagonals, (stack, diagonal, keep, send, packed) = refs[:4], refs[4:8], refs[8:]
        for n in range(4):
            start = pl.multiple_of(place(n) * RANK, RANK)
            stack[pl.ds(start, RANK), :] = ins[n][:RANK, :width]
            lane = grams[n][1]
            if lane is None:
                for q in range(RANK // 8):
                    rows = pl.ds(start + 8 * q, 8)
                    diagonal[rows, :] = diagonals[n][RANK:, q * RANK : (q + 1) * RANK]
            else:
                diagonal[pl.ds(start, RANK), :] = diagonals[n][:, lane : lane + RANK]
        symmetric, terms = gram_terms(stack[...])
        gram = symmetric + (terms + terms.T)
        at = 0
        for i in range(3):
            columns = (3 - i) * RANK
            packed[:, at : at + columns] = gram[i * RANK : (i + 1) * RANK, (i + 1) * RANK :]
            at += columns
        core = lax.axis_index("c")
        keep[...] = packed[pl.ds(pl.multiple_of(core * half, half), half), :]
        send[...] = packed[pl.ds(pl.multiple_of((1 - core) * half, half), half), :]

    return call(
        kernel,
        "quad_gram",
        [(4 * RANK, width), (4 * RANK, RANK), (half, 6 * RANK), (half, 6 * RANK)],
        *pieces,
        *(gram for gram, _ in grams),
        scratch=[pltpu.VMEM((RANK, 6 * RANK), F32)],
    )


def quad_merge(own_half, other_half, diagonal, stack, split):
    rows, width = stack.shape
    share = width // 4 if split else width

    def kernel(own_ref, other_ref, diagonal_ref, stack_ref, *outs):
        core = lax.axis_index("c")
        first = core == 0
        own_half = own_ref[...]
        other_half = other_ref[...]
        packed = jnp.concatenate(
            [
                jnp.where(first, own_half, other_half),
                jnp.where(first, other_half, own_half),
            ],
            0,
        )
        at = 0
        found = {}
        for i in range(4):
            found[i, i] = diagonal_ref[i * RANK : (i + 1) * RANK, :]
            for j in range(i + 1, 4):
                found[i, j] = packed[:, at : at + RANK]
                found[j, i] = found[i, j].T
                at += RANK
        gram = jnp.concatenate(
            [jnp.concatenate([found[i, j] for j in range(4)], 1) for i in range(4)], 0
        )
        weights, merged_gram = two_levels(gram)
        if not split:
            outs[0][...] = product(weights, stack_ref[...])
            return
        x = lax.axis_index("x")
        for s in range(4):
            start = pl.multiple_of((x ^ s) * share, share)
            outs[s][:RANK, :] = product(weights, stack_ref[:, pl.ds(start, share)])
            for q in range(RANK // 8):
                outs[s][RANK:, q * RANK : (q + 1) * RANK] = merged_gram[8 * q : 8 * q + 8]

    shapes = [(RANK + 8, share)] * 4 if split else [(RANK, share)]
    return call(kernel, "quad_merge", shapes, own_half, other_half, diagonal, stack)


def swap(block, axis, bits):
    count = lax.axis_size(axis)
    return lax.ppermute(block, axis, [(i, i ^ bits) for i in range(count)])


def outward(block, distance):
    route = [(i, (i + (distance if i % 2 else -distance)) % 8) for i in range(8)]
    return lax.ppermute(block, "z", route)


def sum_four(block, axis, unit):
    one, two, three = (swap(block, axis, unit * s) for s in (1, 2, 3))
    return (block + one) + (two + three)


def body(factor):
    width = factor.shape[1] // 32
    factor = pltpu.with_memory_space_constraint(factor, pltpu.HBM)
    (near,) = pack(factor, False, width, [(1, 2)])
    other_near = swap(near, "z", 1)
    far, none = pack(factor, False, width, [(3,), (0,)])
    other_far = swap(far, "z", 1)
    none, other_far = after(none, other_far)
    other_none = swap(none, "z", 1)
    own_one, own_two, own_none, own_far = pack(factor, True, width, [(1,), (2,), (0,), (3,)])
    first_own = outward(own_one, 1)
    relay_own = outward(own_two, 1)
    from_near = outward(other_near, 1)

    gram, first_own, relay_own = pair_gram(
        near_gram([own_one, own_two], other_near),
        [own_none, own_far],
        [other_none, other_far],
        [first_own, relay_own],
    )
    second_own = swap(relay_own, "z", 1)
    gram = gram + swap(gram, "c", 1)
    gram = sum_four(gram, "y", 1)
    basis, far, from_near, second_own = pair_solve(
        gram, swap(gram, "z", 1), own_far, other_far, [from_near, second_own]
    )
    second_other = swap(from_near[1:], "z", 1)
    basis_one = outward(basis, 1)
    basis_two = outward(basis, 2)
    far = outward(far, 3)
    pieces = near_merge(
        [basis, basis_one, basis_two],
        [own_none, first_own, second_own],
        [other_none, from_near, second_other],
    )

    def place_z(n):
        where, odd, sign = signs()
        offset = (0, 1, -1, 2)[n]
        return lax.rem(lax.div(where, 2) + sign * offset + 8, 4)

    reach = 4 * width
    lane = 2 * RANK
    stack, diagonal, keep, send = quad_gram(
        [*pieces, far],
        [(basis, lane), (basis_one, lane), (basis_two, lane), (far, reach)],
        reach,
        place_z,
    )
    half = keep + swap(send, "c", 1)
    half = sum_four(half, "y", 1)
    half = half + swap(half, "z", 1)
    half = sum_four(half, "z", 2)
    parts = quad_merge(half, swap(half, "c", 1), diagonal, stack, True)

    pieces = [parts[0]] + [swap(parts[s], "x", s) for s in range(1, 4)]

    def place_x(n):
        return lax.axis_index("x") ^ n

    stack, diagonal, keep, send = quad_gram(
        pieces, [(piece, None) for piece in pieces], width, place_x
    )
    half = keep + swap(send, "c", 1)
    half = sum_four(half, "y", 1)
    half = half + swap(half, "z", 1)
    half = sum_four(half, "z", 2)
    half = sum_four(half, "x", 1)
    (merged,) = quad_merge(half, swap(half, "c", 1), diagonal, stack, False)
    return merged


def solution(mesh):
    split = Mesh(mesh.devices.reshape(4, 2, 4, 8), ("y", "c", "x", "z"))
    return jax.shard_map(
        body,
        mesh=split,
        in_specs=(P(("x", "z"), ("y", "c")),),
        out_specs=P(None, ("y", "c", "x", "z")),
        check_vma=False,
    )
```
